128 devices in a mesh: row: 4 (over y), col: 32 (over z, x, core).
Axes of the slice: x: 4, y: 4, z: 4, core: 2. Of those that a mesh axis runs over, the one named last changes fastest.
Arguments:
- features: bfloat16 [32768, 128], P(('row', 'col')), may hold values from -6 to 6
- weight: bfloat16 [128, 256], replicated, may hold values from -0.5 to 0.5
- cotangent: bfloat16 [32768, 256], P(('row', 'col')), may hold values from -6 to 6
- tile_values: bfloat16 [4, 32, 320, 128, 128], P('row', 'col'), may hold values from -0.1875 to 0.1875
- tile_rows: int32 [4, 32, 320], P('row', 'col'), may hold values from 0 to 63
- tile_cols: int32 [4, 32, 320], P('row', 'col'), may hold values from 0 to 7
- tile_counts: int32 [4, 32], P('row', 'col'), may hold values from 40 to 320, as said below
Outputs:
- output: bfloat16 [32768, 256], P(('row', 'col'))
- grad_features: bfloat16 [32768, 128], P(('row', 'col'))
- grad_weight: float32 [128, 256], replicated
The draws below stay inside these ranges and needn't reach their ends.
Inputs may be any that keep to these rules, and one draw needn't show every extreme that they name: Slots 0 to tile_counts - 1 of a grid cell are live and the rest are ignored; the (row tile, column tile) pairs of a cell's live slots are distinct; some cells hold 320 live slots.
All inputs are finite; a program needn't handle non-finite values.
Results may differ from the reference program's by a relative error of at most 0.0049.
Values may be sent and summed in bfloat16 or wider, within the bound.
No kernel may reach another device: no remote copies, remote signals or barrier semaphores. Data moves between devices by JAX's collectives and lax.ppermute only.
A program may use at most 128 MiB of HBM per device.

```python
import jax
import jax.numpy as jnp
from jax import lax

F = 128
H = 256
TILE = 128
NB = 256
GRID_ROWS = 4
GRID_COLS = 32
NODES = 32768
RT = 64
CT = 8
TMAX = 320


def tile_slots(key):
    folded = jax.random.fold_in(key, 7)
    device_keys = jax.random.split(folded, GRID_ROWS * GRID_COLS)

    def one_device(device_key):
        return jax.random.permutation(device_key, RT * CT)[:TMAX]
    slot_ids = jax.vmap(one_device)(device_keys)
    return slot_ids.reshape(GRID_ROWS, GRID_COLS, TMAX).astype(jnp.int32)


def draw_tile_rows(key, part):
    return tile_slots(key) // CT


def draw_tile_cols(key, part):
    return tile_slots(key) % CT


def draw_tile_counts(key, part):
    folded = jax.random.fold_in(key, 11)
    key_counts, key_heavy = jax.random.split(folded)
    counts = jax.random.randint(key_counts, (GRID_ROWS * GRID_COLS,), TMAX // 8, TMAX // 2 + 1)
    heavy_ids = jax.random.permutation(key_heavy, GRID_ROWS * GRID_COLS)[:4]
    counts = counts.at[heavy_ids].set(TMAX)
    return counts.reshape(GRID_ROWS, GRID_COLS).astype(jnp.int32)


def shard_levels(own_key, dims, cuts, smallest, top_value):
    factor_of, own = 1.0, jax.random.fold_in(own_key, 6)
    for axis_at, blocks in cuts:
        heights = jnp.exp(jax.random.uniform(jax.random.fold_in(own, axis_at), (blocks,), jnp.float32, smallest / len(cuts), top_value / len(cuts)))
        factor_of = factor_of * jnp.repeat(heights, dims[axis_at] // blocks).reshape([-1 if axis == axis_at else 1 for axis in range(len(dims))])
    return factor_of


def normal_values(own_key, dims, scale, bound, pieces=(), dtype=jnp.bfloat16):
    entries = scale * jax.random.normal(own_key, dims, jnp.float32)
    if pieces:
        entries = entries * shard_levels(own_key, dims, pieces, -0.22, 0.18)
    return jnp.clip(entries, -bound, bound).astype(dtype)


def setup_inputs(seed: int = 0) -> dict:
    keys = jax.random.split(jax.random.key(seed), 8)
    features = normal_values(keys[0], (NODES, F), 1.0, 6.0, ((0, 128),))
    weight = normal_values(keys[1], (F, H), F ** -0.5, 0.5)
    cotangent = normal_values(keys[2], (NODES, H), 1.0, 6.0, ((0, 128),))
    tile_values = normal_values(keys[3], (GRID_ROWS, GRID_COLS, TMAX, TILE, TILE), ((5 * TILE * GRID_COLS * TMAX / (16 * RT)) ** -0.5), 0.1875, ((0, 4), (1, 32)))
    tile_rows = draw_tile_rows(jax.random.fold_in(keys[7], 71), 0)
    tile_cols = draw_tile_cols(jax.random.fold_in(keys[7], 71), 0)
    tile_counts = draw_tile_counts(jax.random.fold_in(keys[7], 71), 0)
    return {"features": features, "weight": weight, "cotangent": cotangent, "tile_values": tile_values, "tile_rows": tile_rows, "tile_cols": tile_cols, "tile_counts": tile_counts}


def silu_slope(values):
    sigmoid_part = jax.nn.sigmoid(values)
    return sigmoid_part * (1.0 + values * (1.0 - sigmoid_part))


def tile_product(slot_values, slot_rows, slot_cols, live_count, source, out_tiles):
    live_mask = jnp.arange(slot_values.shape[0]) < live_count
    weights = jnp.where(live_mask[:, None, None], slot_values.astype(jnp.float32), jnp.zeros((), jnp.float32))
    picked = jnp.take(source, slot_cols, axis=0).astype(jnp.float32)
    products = jnp.einsum('tij,tjh->tih', weights, picked, precision=lax.Precision.HIGHEST)
    empty = jnp.zeros((out_tiles,) + products.shape[1:], jnp.float32)
    return empty.at[slot_rows].add(products)


def reference(features, weight, cotangent, tile_values, tile_rows, tile_cols, tile_counts):
    blocks = features.reshape(GRID_ROWS, GRID_COLS, NB, F)
    sources = jnp.swapaxes(blocks, 0, 1).reshape(GRID_COLS, CT, TILE, F)

    def forward_row(row_args):
        def add_block(running, block_args):
            block_values, block_rows, block_cols, block_count, block_source = block_args
            return running + tile_product(block_values, block_rows, block_cols, block_count, block_source, RT), None

        running, unused = lax.scan(add_block, jnp.zeros((RT, TILE, F), jnp.float32), tuple(row_args) + (sources,))
        return running

    aggregated = lax.map(forward_row, (tile_values, tile_rows, tile_cols, tile_counts)).reshape(NODES, F)
    summed = jnp.dot(aggregated, weight.astype(jnp.float32), precision=lax.Precision.HIGHEST)
    output = jax.nn.silu(summed).astype(jnp.bfloat16)
    grad_summed = (cotangent.astype(jnp.float32) * silu_slope(summed)).astype(jnp.bfloat16)
    grad_sources = grad_summed.reshape(GRID_ROWS, RT, TILE, H)

    def backward_col(col_index):
        def add_block(running, row_index):
            flipped = jnp.swapaxes(tile_values[row_index, col_index], 1, 2)
            term = tile_product(flipped, tile_cols[row_index, col_index], tile_rows[row_index, col_index], tile_counts[row_index, col_index], grad_sources[row_index], CT)
            return running + term, None

        running, unused = lax.scan(add_block, jnp.zeros((CT, TILE, H), jnp.float32), jnp.arange(GRID_ROWS))
        return running

    grad_cols = lax.map(backward_col, jnp.arange(GRID_COLS))
    grad_mixed = jnp.swapaxes(grad_cols.reshape(GRID_COLS, GRID_ROWS, NB, H), 0, 1).reshape(NODES, H)
    grad_features = jnp.dot(grad_mixed, weight.astype(jnp.float32).T, precision=lax.Precision.HIGHEST).astype(jnp.bfloat16)
    grad_weight = jnp.dot(features.astype(jnp.float32).T, grad_mixed, precision=lax.Precision.HIGHEST) * (NODES ** -0.5)
    return output, grad_features, grad_weight
```

```python
import functools

import jax
import jax.numpy as jnp
from jax import lax
from jax.experimental import pallas as pl
from jax.experimental.pallas import tpu as pltpu
from jax.sharding import PartitionSpec as P

BF = jnp.bfloat16
F32 = jnp.float32
VM = pl.BlockSpec(memory_space=pltpu.VMEM)
SM = pl.BlockSpec(memory_space=pltpu.SMEM)
PARAMS = pltpu.CompilerParams(vmem_limit_bytes=24 << 20)

FWD_TILES = 4
BWD_UNROLL = 4


def sds(shape, dtype):
    return jax.ShapeDtypeStruct(shape, dtype)


def dot(a, b):
    return jnp.dot(a, b, preferred_element_type=F32)


def split(v):
    high = v.astype(BF)
    return high, (v - high.astype(F32)).astype(BF)


def joined(ref, at):
    return ref[at].astype(F32) + ref[at + 1].astype(F32)


def tile(values, slot):
    found = values[jnp.maximum(slot, 0)]
    return jnp.where(slot >= 0, found, jnp.zeros_like(found))


def forward_kernel(half, table, values, x0, x1, x2, x3, out):
    sources = (x0, x1, x2, x3)
    rows = FWD_TILES * 128

    @pl.loop(0, 32 // FWD_TILES)
    def _(step):
        total = None
        for k in range(4):
            left = []
            for r in range(FWD_TILES):
                base = (half * 32 + step * FWD_TILES + r) * 8 + 2 * k
                left.append(
                    jnp.concatenate(
                        [tile(values, table[base]), tile(values, table[base + 1])], axis=1
                    )
                )
            term = dot(jnp.concatenate(left, axis=0), sources[k][...])
            total = term if total is None else total + term
        out[pl.ds(pl.multiple_of(step * rows, rows), rows), :] = total.astype(out.dtype)


def forward_half(half, dtype, table, values, sources):
    return pl.pallas_call(
        functools.partial(forward_kernel, half),
        out_shape=sds((4096, 128), dtype),
        in_specs=[SM] + [VM] * 5,
        out_specs=VM,
        name=f"forward_{half}",
        cost_estimate=pl.CostEstimate(
            flops=2 * 4096 * 1024 * 128, bytes_accessed=6 << 20, transcendentals=0
        ),
        compiler_params=PARAMS,
    )(table, values, *sources)


def first_sum_kernel(own, got, mine, s1, s2, s3):
    for a, out in enumerate((mine, s1, s2, s3)):
        part = pl.ds(a * 1024, 1024)
        out[...] = (own[part, :] + got[part, :].astype(F32)).astype(out.dtype)


def first_sum(own, got):
    return pl.pallas_call(
        first_sum_kernel,
        out_shape=(sds((1024, 128), F32),) + (sds((1024, 128), BF),) * 3,
        in_specs=[VM] * 2,
        out_specs=(VM,) * 4,
        name="first_sum",
        compiler_params=PARAMS,
    )(own, got)


def second_sum_kernel(own, g1, g2, g3, mine, s1, s2, s3):
    for b, out in enumerate((mine, s1, s2, s3)):
        part = pl.ds(b * 256, 256)
        total = own[part, :] + g1[part, :].astype(F32)
        total = total + g2[part, :].astype(F32) + g3[part, :].astype(F32)
        out[...] = total.astype(out.dtype)


def second_sum(own, got):
    return pl.pallas_call(
        second_sum_kernel,
        out_shape=(sds((256, 128), F32),) + (sds((256, 128), BF),) * 3,
        in_specs=[VM] * 4,
        out_specs=(VM,) * 4,
        name="second_sum",
        compiler_params=PARAMS,
    )(own, *got)


def middle_kernel(own, g1, g2, g3, weight, cotangent, out, message):
    mixed = own[...] + g1[...].astype(F32) + g2[...].astype(F32) + g3[...].astype(F32)
    high, low = split(mixed)
    w = weight[...]
    summed = dot(high, w) + dot(low, w)
    gate = 1.0 / (1.0 + jnp.exp(-summed))
    out[...] = (summed * gate).astype(BF)
    slope = gate * (1.0 + summed * (1.0 - gate))
    grad = (cotangent[...].astype(F32) * slope).astype(BF)
    back = lax.dot_general(w, grad, (((1,), (1,)), ((), ())), preferred_element_type=F32)
    message[0] = back.astype(BF)
    over_rows = (((0,), (0,)), ((), ()))
    term = lax.dot_general(high, grad, over_rows, preferred_element_type=F32)
    term = term + lax.dot_general(low, grad, over_rows, preferred_element_type=F32)
    message[1], message[2] = split(term)


def middle(own, got, weight, cotangent):
    return pl.pallas_call(
        middle_kernel,
        out_shape=(sds((256, 256), BF), sds((3, 128, 256), BF)),
        in_specs=[VM] * 6,
        out_specs=(VM,) * 2,
        name="middle",
        compiler_params=PARAMS,
    )(own, *got, weight, cotangent)


def ring_sum(own, g1, g2, g3, at):
    return (joined(own, at) + joined(g2, at)) + (joined(g1, at) + joined(g3, at))


def gather_kernel(own, g1, g2, g3, message):
    for b, ref in enumerate((own, g1, g2, g3)):
        message[b] = ref[0]
    message[4], message[5] = split(ring_sum(own, g1, g2, g3, 1))


def gather_step(own, got):
    return pl.pallas_call(
        gather_kernel,
        out_shape=sds((6, 128, 256), BF),
        in_specs=[VM] * 4,
        out_specs=VM,
        name="gather_step",
        compiler_params=PARAMS,
    )(own, *got)


def backward_tiles(half, table, values, parts, emit):
    for q in range(4):
        total = jnp.zeros((128, 256), F32)
        for a, part in enumerate(parts):
            for b in range(4):
                base = (half * 32 + a * 8 + b * 2) * 8 + 2 * q
                upper = [tile(values, table[base]), tile(values, table[base + 1])]
                lower = [tile(values, table[base + 8]), tile(values, table[base + 9])]
                block = jnp.concatenate(
                    [jnp.concatenate(upper, axis=1), jnp.concatenate(lower, axis=1)], axis=0
                )
                total = total + dot(part[b], block)
        emit(q, total)


def backward_own_kernel(table, values, p0, p1, p2, p3, out, term):
    def emit(q, total):
        out[q] = total

    backward_tiles(1, table, values, (p0, p1, p2, p3), emit)
    term[...] = ring_sum(p0, p1, p2, p3, 4)


def backward_other_kernel(table, values, p0, p1, p2, p3, partial, term, own, own_term, s1, s2, s3):
    sends = (s1, s2, s3)

    def emit(q, total):
        total = total + partial[q]
        if q == 0:
            own[...] = total
        else:
            sends[q - 1][0] = total.astype(BF)

    backward_tiles(0, table, values, (p0, p1, p2, p3), emit)
    high, low = split(term[...] + ring_sum(p0, p1, p2, p3, 4))
    own_term[0] = high
    own_term[1] = low
    for out in sends:
        out[1] = high
        out[2] = low


BACK_COST = pl.CostEstimate(
    flops=2 * 4096 * 1024 * 128, bytes_accessed=6 << 20, transcendentals=0
)


def backward_own(table, values, parts):
    return pl.pallas_call(
        backward_own_kernel,
        out_shape=(sds((4, 128, 256), F32), sds((128, 256), F32)),
        in_specs=[SM] + [VM] * 5,
        out_specs=(VM,) * 2,
        name="backward_own",
        cost_estimate=BACK_COST,
        compiler_params=PARAMS,
    )(table, values, *parts)


def backward_other(table, values, parts, partial, term):
    return pl.pallas_call(
        backward_other_kernel,
        out_shape=(sds((128, 256), F32), sds((2, 128, 256), BF)) + (sds((3, 128, 256), BF),) * 3,
        in_specs=[SM] + [VM] * 7,
        out_specs=(VM,) * 5,
        name="backward_other",
        cost_estimate=BACK_COST,
        compiler_params=PARAMS,
    )(table, values, *parts, partial, term)


def finish_kernel(scale, own, own_term, g1, g2, g3, grad_in, grad_weight):
    total = own[...] + g1[0].astype(F32) + g2[0].astype(F32) + g3[0].astype(F32)
    grad_in[...] = total.T.astype(BF)
    term = (joined(own_term, 0) + joined(g2, 1)) + (joined(g1, 1) + joined(g3, 1))
    grad_weight[...] = term * scale


def finish(scale, own, own_term, got):
    return pl.pallas_call(
        functools.partial(finish_kernel, scale),
        out_shape=(sds((256, 128), BF), sds((128, 256), F32)),
        in_specs=[VM] * 5,
        out_specs=(VM,) * 2,
        name="finish",
        compiler_params=PARAMS,
    )(own, own_term, *got)


def row_shift(value, k):
    return lax.ppermute(value, "row", [(i, (i + k) % 4) for i in range(4)])


def swap_cores(value):
    return lax.ppermute(value, "col", [(j, j ^ 1) for j in range(32)])


def chip_shift(value, k, x_core):
    pairs = []
    for z in range(4):
        for x in range(4):
            for core in range(2):
                if core == x_core:
                    to = (z, (x + k) % 4)
                else:
                    to = ((z + k) % 4, x)
                pairs.append(((z * 4 + x) * 2 + core, (to[0] * 4 + to[1]) * 2 + core))
    return lax.ppermute(value, "col", pairs)


def slot_table(slot_rows, slot_cols, live_count):
    row, col = lax.axis_index("row"), lax.axis_index("col")
    core, x, z = col & 1, (col >> 1) & 3, col >> 3
    block = slot_rows >> 1
    parity = block & 1
    dx = (((block >> 1) & 3) - x) & 3
    dz = ((block >> 3) - z) & 3
    even = parity == 0
    a = jnp.where(even, dx, dz)
    b = jnp.where(even, dz, dx)
    half = (parity == core).astype(jnp.int32)
    place = half * 32 + a * 8 + b * 2 + (slot_rows & 1)
    source = ((row - (slot_cols >> 1)) & 3) * 2 + (slot_cols & 1)
    slots = jnp.arange(slot_rows.shape[0], dtype=jnp.int32)
    key = jnp.where(slots < live_count, place * 8 + source, -1)
    hits = key[:, None] == jnp.arange(512, dtype=jnp.int32)[None, :]
    return jnp.max(jnp.where(hits, slots[:, None], -1), axis=0)


def local(features, weight, cotangent, tile_values, tile_rows, tile_cols, tile_counts):
    values = tile_values[0, 0]
    table = slot_table(tile_rows[0, 0], tile_cols[0, 0], tile_counts[0, 0])
    sources = [features] + [row_shift(features, k) for k in (1, 2, 3)]
    other = swap_cores(forward_half(0, BF, table, values, sources))
    kept = forward_half(1, F32, table, values, sources)
    own, *sends = first_sum(kept, other)
    got = [chip_shift(v, k, 0) for k, v in zip((1, 2, 3), sends)]
    own, *sends = second_sum(own, got)
    got = [chip_shift(v, k, 1) for k, v in zip((1, 2, 3), sends)]
    output, message = middle(own, got, weight, cotangent)
    got = [chip_shift(message, -k, 1) for k in (1, 2, 3)]
    message = gather_step(message, got)
    mine = [message] + [chip_shift(message, -k, 0) for k in (1, 2, 3)]
    others = [swap_cores(v) for v in mine]
    partial, term = backward_own(table, values, mine)
    own, own_term, *sends = backward_other(table, values, others, partial, term)
    got = [row_shift(v, -k) for k, v in zip((1, 2, 3), sends)]
    grad_in, grad_weight = finish(32768.0 ** -0.5, own, own_term, got)
    return output, grad_in, grad_weight


def solution(mesh):
    placed = (
        P(("row", "col"), None),
        P(),
        P(("row", "col"), None),
        P("row", "col", None, None, None),
        P("row", "col", None),
        P("row", "col", None),
        P("row", "col"),
    )
    return jax.shard_map(
        local,
        mesh=mesh,
        in_specs=placed,
        out_specs=(P(("row", "col"), None), P(("row", "col"), None), P()),
        check_vma=False,
    )
```

```python
import functools

import jax
import jax.numpy as jnp
from jax import lax
from jax.experimental import pallas as pl
from jax.experimental.pallas import tpu as pltpu
from jax.sharding import PartitionSpec as P

BF = jnp.bfloat16
F32 = jnp.float32
VM = pl.BlockSpec(memory_space=pltpu.VMEM)
SM = pl.BlockSpec(memory_space=pltpu.SMEM)
HB = pl.BlockSpec(memory_space=pltpu.HBM)
AN = pl.BlockSpec(memory_space=pl.ANY)
PARAMS = pltpu.CompilerParams(vmem_limit_bytes=24 << 20)

FWD_TILES = 4
COL_TERMS = 2
ROW_TERMS = 2


def sds(shape, dtype):
    return jax.ShapeDtypeStruct(shape, dtype)


def dot(a, b):
    return jnp.dot(a, b, preferred_element_type=F32)


def split(v, terms=2):
    high = v.astype(BF)
    if terms == 1:
        return (high,)
    return high, (v - high.astype(F32)).astype(BF)


def joined(ref, at, terms=2):
    high = ref[at].astype(F32)
    return high if terms == 1 else high + ref[at + 1].astype(F32)


def tile(values, slot):
    found = values[jnp.maximum(slot, 0)]
    return jnp.where(slot >= 0, found, jnp.zeros_like(found))


def load_kernel(values, features, rows_in, cols_in, live, held, own, table, slot_rows, slot_cols, sem):
    pairs = ((rows_in, slot_rows), (cols_in, slot_cols))
    small = [pltpu.make_async_copy(*pair, sem.at[2 + n]) for n, pair in enumerate(pairs)]
    copies = [
        pltpu.make_async_copy(values, held, sem.at[0]),
        pltpu.make_async_copy(features, own, sem.at[1]),
    ]
    for copy in small + copies:
        copy.start()
    row, col = lax.axis_index("row"), lax.axis_index("col")
    core, x, z = col & 1, (col >> 1) & 3, col >> 3

    def clear(step, carry):
        for u in range(16):
            table[step * 16 + u] = -1
        return carry

    lax.fori_loop(0, 32, clear, 0)
    for copy in small:
        copy.wait()

    def place(slot):
        tile_row, tile_col = slot_rows[0, 0, slot], slot_cols[0, 0, slot]
        parity = (tile_row >> 1) & 1
        dx = ((tile_row >> 2) - x) & 3
        dz = ((tile_row >> 4) - z) & 3
        a = jnp.where(parity == 0, dx, dz)
        b = jnp.where(parity == 0, dz, dx)
        half = 1 - (parity ^ core)
        source = ((row - (tile_col >> 1)) & 3) * 2 + (tile_col & 1)
        table[(half * 32 + a * 8 + b * 2 + (tile_row & 1)) * 8 + source] = slot

    count = live[0, 0]

    def place_four(step, carry):
        for u in range(4):
            place(step * 4 + u)
        return carry

    def place_one(slot, carry):
        place(slot)
        return carry

    lax.fori_loop(0, count >> 2, place_four, 0)
    lax.fori_loop((count >> 2) << 2, count, place_one, 0)
    for copy in copies:
        copy.wait()


def load(values, features, slot_rows, slot_cols, live):
    given = (values, features, slot_rows, slot_cols)
    given = [pltpu.with_memory_space_constraint(value, pltpu.HBM) for value in given]
    slots = values.shape[0]
    return pl.pallas_call(
        load_kernel,
        out_shape=(sds(values.shape, BF), sds(features.shape, BF), pltpu.SMEM((512,), jnp.int32)),
        in_specs=[HB] * 4 + [SM],
        out_specs=(VM, VM, SM),
        scratch_shapes=[
            pltpu.SMEM((1, 1, slots), jnp.int32),
            pltpu.SMEM((1, 1, slots), jnp.int32),
            pltpu.SemaphoreType.DMA((4,)),
        ],
        name="load",
        cost_estimate=pl.CostEstimate(flops=0, bytes_accessed=11 << 20, transcendentals=0),
        compiler_params=PARAMS,
    )(*given, live)


def forward_kernel(start, steps, table, values, x0, x1, x2, x3, out):
    sources = (x0, x1, x2, x3)
    rows = FWD_TILES * 128
    for step in range(steps):
        total = None
        for k in range(4):
            left = []
            for r in range(FWD_TILES):
                base = (start + step * FWD_TILES + r) * 8 + 2 * k
                left.append(
                    jnp.concatenate(
                        [tile(values, table[base]), tile(values, table[base + 1])], axis=1
                    )
                )
            term = dot(jnp.concatenate(left, axis=0), sources[k][...])
            total = term if total is None else total + term
        out[step * rows : (step + 1) * rows, :] = total.astype(out.dtype)


def forward(name, start, count, dtype, table, values, sources):
    return pl.pallas_call(
        functools.partial(forward_kernel, start, count // FWD_TILES),
        out_shape=sds((count * 128, 128), dtype),
        in_specs=[SM] + [VM] * 5,
        out_specs=VM,
        name=name,
        cost_estimate=pl.CostEstimate(
            flops=2 * count * 128 * 1024 * 128, bytes_accessed=count << 15, transcendentals=0
        ),
        compiler_params=PARAMS,
    )(table, values, *sources)


def first_sum_kernel(kept, got, s1, s2, s3):
    for a, out in enumerate((s1, s2, s3)):
        total = kept[a * 1024 : a * 1024 + 1024, :] + got[a * 1024 + 1024 : a * 1024 + 2048, :].astype(F32)
        out[...] = total.astype(BF)


def first_sum(kept, got):
    return pl.pallas_call(
        first_sum_kernel,
        out_shape=(sds((1024, 128), BF),) * 3,
        in_specs=[VM] * 2,
        out_specs=(VM,) * 3,
        name="first_sum",
        compiler_params=PARAMS,
    )(kept, got)


def second_sum_kernel(own, other, g1, g2, g3, mine, s1, s2, s3):
    for b, out in enumerate((mine, s1, s2, s3)):
        part = pl.ds(b * 256, 256)
        total = own[part, :] + other[part, :].astype(F32) + g1[part, :].astype(F32)
        total = total + g2[part, :].astype(F32) + g3[part, :].astype(F32)
        out[...] = total.astype(out.dtype)


def second_sum(own, other, got):
    return pl.pallas_call(
        second_sum_kernel,
        out_shape=(sds((256, 128), F32),) + (sds((256, 128), BF),) * 3,
        in_specs=[VM] * 5,
        out_specs=(VM,) * 4,
        name="second_sum",
        compiler_params=PARAMS,
    )(own, other, *got)


def middle_kernel(own, g1, g2, g3, weight, cotangent, out, message):
    mixed = own[...] + g1[...].astype(F32) + g2[...].astype(F32) + g3[...].astype(F32)
    high, low = split(mixed)
    w = weight[...]
    summed = dot(high, w) + dot(low, w)
    gate = 1.0 / (1.0 + jnp.exp(-summed))
    out[...] = (summed * gate).astype(BF)
    slope = gate * (1.0 + summed * (1.0 - gate))
    grad = (cotangent[...].astype(F32) * slope).astype(BF)
    back = lax.dot_general(w, grad, (((1,), (1,)), ((), ())), preferred_element_type=F32)
    message[0] = back.astype(BF)
    over_rows = (((0,), (0,)), ((), ()))
    term = lax.dot_general(high, grad, over_rows, preferred_element_type=F32)
    term = term + lax.dot_general(low, grad, over_rows, preferred_element_type=F32)
    message[1], message[2] = split(term)


def middle(own, got, weight, cotangent):
    return pl.pallas_call(
        middle_kernel,
        out_shape=(sds((256, 256), BF), sds((3, 128, 256), BF)),
        in_specs=[VM] * 6,
        out_specs=(VM,) * 2,
        name="middle",
        compiler_params=PARAMS,
    )(own, *got, weight, cotangent)


def ring_sum(own, g1, g2, g3, at, terms=2):
    own, g1, g2, g3 = [joined(ref, at, terms) for ref in (own, g1, g2, g3)]
    return (own + g2) + (g1 + g3)


def gather_kernel(own, g1, g2, g3, message):
    for b, ref in enumerate((own, g1, g2, g3)):
        message[b] = ref[0]
    for n, term in enumerate(split(ring_sum(own, g1, g2, g3, 1), COL_TERMS)):
        message[4 + n] = term


def gather_step(own, got):
    return pl.pallas_call(
        gather_kernel,
        out_shape=sds((4 + COL_TERMS, 128, 256), BF),
        in_specs=[VM] * 4,
        out_specs=VM,
        name="gather_step",
        compiler_params=PARAMS,
    )(own, *got)


def backward_tiles(half, a, q, table, values, part, total):
    for b in range(4):
        base = (half * 32 + a * 8 + b * 2) * 8 + 2 * q
        upper = [tile(values, table[base]), tile(values, table[base + 1])]
        lower = [tile(values, table[base + 8]), tile(values, table[base + 9])]
        block = jnp.concatenate(
            [jnp.concatenate(upper, axis=1), jnp.concatenate(lower, axis=1)], axis=0
        )
        term = dot(part[b], block)
        total = term if total is None else total + term
    return total


def backward_kernel(half, offsets, first, table, values, *refs):
    parts, out = refs[: len(offsets)], refs[-1]
    for q in range(4):
        total = None if first else refs[len(offsets)][q]
        for a, part in zip(offsets, parts):
            total = backward_tiles(half, a, q, table, values, part, total)
        out[q] = total


BACK_COST = pl.CostEstimate(flops=1, bytes_accessed=1, transcendentals=0)


def backward(half, offsets, table, values, parts, partial):
    given = () if partial is None else (partial,)
    return pl.pallas_call(
        functools.partial(backward_kernel, half, offsets, partial is None),
        out_shape=sds((4, 128, 256), F32),
        in_specs=[SM] + [VM] * (1 + len(parts) + len(given)),
        out_specs=VM,
        name=f"backward_{half}_{offsets[0]}",
        cost_estimate=BACK_COST,
        compiler_params=PARAMS,
    )(table, values, *parts, *given)


def tie_kernel(*refs):
    del refs


def tie(values, after):
    return pl.pallas_call(
        tie_kernel,
        out_shape=[sds(value.shape, value.dtype) for value in values],
        in_specs=[AN] * (len(values) + 1),
        out_specs=[AN] * len(values),
        input_output_aliases={n: n for n in range(len(values))},
        name="tie",
        compiler_params=PARAMS,
    )(*values, after)


def last_kernel(half, offsets, table, values, p0, p1, p2, p3, o0, o1, o2, o3, partial, own, own_term, s1, s2, s3):
    sends = (s1, s2, s3)
    parts = [(o0, o1, o2, o3)[a] for a in offsets]
    term = ring_sum(p0, p1, p2, p3, 4, COL_TERMS) + ring_sum(o0, o1, o2, o3, 4, COL_TERMS)
    for n, term in enumerate(split(term, ROW_TERMS)):
        own_term[n] = term
        for out in sends:
            out[1 + n] = term
    for q in range(4):
        total = partial[q]
        for a, part in zip(offsets, parts):
            total = backward_tiles(half, a, q, table, values, part, total)
        if q == 0:
            own[...] = total
        else:
            sends[q - 1][0] = total.astype(BF)


def last(half, offsets, table, values, mine, others, partial):
    return pl.pallas_call(
        functools.partial(last_kernel, half, offsets),
        out_shape=(sds((128, 256), F32), sds((ROW_TERMS, 128, 256), BF))
        + (sds((1 + ROW_TERMS, 128, 256), BF),) * 3,
        in_specs=[SM] + [VM] * 10,
        out_specs=(VM,) * 5,
        name="backward_last",
        cost_estimate=BACK_COST,
        compiler_params=PARAMS,
    )(table, values, *mine, *others, partial)


def finish_kernel(scale, own, own_term, g1, g2, g3, grad_in, grad_weight):
    total = own[...] + g1[0].astype(F32) + g2[0].astype(F32) + g3[0].astype(F32)
    grad_in[...] = total.T.astype(BF)
    g1, g2, g3 = [joined(ref, 1, ROW_TERMS) for ref in (g1, g2, g3)]
    term = (joined(own_term, 0, ROW_TERMS) + g2) + (g1 + g3)
    grad_weight[...] = term * scale


def finish(scale, own, own_term, got):
    return pl.pallas_call(
        functools.partial(finish_kernel, scale),
        out_shape=(sds((256, 128), BF), sds((128, 256), F32)),
        in_specs=[VM] * 5,
        out_specs=(VM,) * 2,
        name="finish",
        compiler_params=PARAMS,
    )(own, own_term, *got)


def row_shift(value, k):
    return lax.ppermute(value, "row", [(i, (i + k) % 4) for i in range(4)])


def swap_cores(value):
    return lax.ppermute(value, "col", [(j, j ^ 1) for j in range(32)])


def chip_shift(value, k, x_core):
    pairs = []
    for z in range(4):
        for x in range(4):
            for core in range(2):
                if core == x_core:
                    to = (z, (x + k) % 4)
                else:
                    to = ((z + k) % 4, x)
                pairs.append(((z * 4 + x) * 2 + core, (to[0] * 4 + to[1]) * 2 + core))
    return lax.ppermute(value, "col", pairs)


def local(features, weight, cotangent, tile_values, tile_rows, tile_cols, tile_counts):
    shifted = [row_shift(features, k) for k in (1, 2, 3)]
    values, own_features, table = load(
        tile_values[0, 0], features, tile_rows, tile_cols, tile_counts
    )
    sources = [own_features] + shifted
    other = swap_cores(forward("forward_other", 0, 32, BF, table, values, sources))
    kept = forward("forward_sent", 40, 24, F32, table, values, sources)
    sends = first_sum(kept, other)
    got = [chip_shift(v, k, 0) for k, v in zip((1, 2, 3), sends)]
    kept = forward("forward_kept", 32, 8, F32, table, values, sources)
    own, *sends = second_sum(kept, other, got)
    got = [chip_shift(v, k, 1) for k, v in zip((1, 2, 3), sends)]
    output, message = middle(own, got, weight, cotangent)
    got = [chip_shift(message, -k, 1) for k in (1, 2, 3)]
    message = gather_step(message, got)
    p0, p1, p2, p3 = [message] + [chip_shift(message, -k, 0) for k in (1, 2, 3)]
    o0 = swap_cores(p0)
    partial = backward(1, (0,), table, values, (p0,), None)
    partial = backward(0, (0,), table, values, (o0,), partial)
    p1, p2, p3 = tie((p1, p2, p3), partial)
    o1, o2, o3 = [swap_cores(v) for v in (p1, p2, p3)]
    partial = backward(1, (1, 2, 3), table, values, (p1, p2, p3), partial)
    mine, others = (p0, p1, p2, p3), (o0, o1, o2, o3)
    own, own_term, *sends = last(0, (1, 2, 3), table, values, mine, others, partial)
    got = [row_shift(v, -k) for k, v in zip((1, 2, 3), sends)]
    grad_in, grad_weight = finish(32768.0 ** -0.5, own, own_term, got)
    return output, grad_in, grad_weight


def solution(mesh):
    placed = (
        P(("row", "col"), None),
        P(),
        P(("row", "col"), None),
        P("row", "col", None, None, None),
        P("row", "col", None),
        P("row", "col", None),
        P("row", "col"),
    )
    return jax.shard_map(
        local,
        mesh=mesh,
        in_specs=placed,
        out_specs=(P(("row", "col"), None), P(("row", "col"), None), P()),
        check_vma=False,
    )
```

```python
import functools

import jax
import jax.numpy as jnp
from jax import lax
from jax.experimental import pallas as pl
from jax.experimental.pallas import tpu as pltpu
from jax.sharding import PartitionSpec as P

BF = jnp.bfloat16
F32 = jnp.float32
VM = pl.BlockSpec(memory_space=pltpu.VMEM)
SM = pl.BlockSpec(memory_space=pltpu.SMEM)
HB = pl.BlockSpec(memory_space=pltpu.HBM)
AN = pl.BlockSpec(memory_space=pl.ANY)
PARAMS = pltpu.CompilerParams(vmem_limit_bytes=24 << 20)

FWD_TILES = 4
COL_TERMS = 1
ROW_TERMS = 1


def sds(shape, dtype):
    return jax.ShapeDtypeStruct(shape, dtype)


def dot(a, b):
    return jnp.dot(a, b, preferred_element_type=F32)


def split(v, terms=2):
    high = v.astype(BF)
    if terms == 1:
        return (high,)
    return high, (v - high.astype(F32)).astype(BF)


def joined(ref, at, terms=2):
    high = ref[at].astype(F32)
    return high if terms == 1 else high + ref[at + 1].astype(F32)


def tile(values, slot):
    found = values[jnp.maximum(slot, 0)]
    return jnp.where(slot >= 0, found, jnp.zeros_like(found))


def load_kernel(values, features, rows_in, cols_in, live, held, own, table, slot_rows, slot_cols, sem):
    pairs = ((rows_in, slot_rows), (cols_in, slot_cols))
    small = [pltpu.make_async_copy(*pair, sem.at[2 + n]) for n, pair in enumerate(pairs)]
    copies = [
        pltpu.make_async_copy(values, held, sem.at[0]),
        pltpu.make_async_copy(features, own, sem.at[1]),
    ]
    for copy in small + copies:
        copy.start()
    row, col = lax.axis_index("row"), lax.axis_index("col")
    core, x, z = col & 1, (col >> 1) & 3, col >> 3

    def clear(step, carry):
        for u in range(16):
            table[step * 16 + u] = -1
        return carry

    lax.fori_loop(0, 32, clear, 0)
    for copy in small:
        copy.wait()

    def place(slot):
        tile_row, tile_col = slot_rows[0, 0, slot], slot_cols[0, 0, slot]
        parity = (tile_row >> 1) & 1
        dx = ((tile_row >> 2) - x) & 3
        dz = ((tile_row >> 4) - z) & 3
        a = jnp.where(parity == 0, dx, dz)
        b = jnp.where(parity == 0, dz, dx)
        half = 1 - (parity ^ core)
        source = ((row - (tile_col >> 1)) & 3) * 2 + (tile_col & 1)
        table[(half * 32 + a * 8 + b * 2 + (tile_row & 1)) * 8 + source] = slot

    count = live[0, 0]

    def place_four(step, carry):
        for u in range(4):
            place(step * 4 + u)
        return carry

    def place_one(slot, carry):
        place(slot)
        return carry

    lax.fori_loop(0, count >> 2, place_four, 0)
    lax.fori_loop((count >> 2) << 2, count, place_one, 0)
    for copy in copies:
        copy.wait()


def load(values, features, slot_rows, slot_cols, live):
    given = (values, features, slot_rows, slot_cols)
    given = [pltpu.with_memory_space_constraint(value, pltpu.HBM) for value in given]
    slots = values.shape[0]
    return pl.pallas_call(
        load_kernel,
        out_shape=(sds(values.shape, BF), sds(features.shape, BF), pltpu.SMEM((512,), jnp.int32)),
        in_specs=[HB] * 4 + [SM],
        out_specs=(VM, VM, SM),
        scratch_shapes=[
            pltpu.SMEM((1, 1, slots), jnp.int32),
            pltpu.SMEM((1, 1, slots), jnp.int32),
            pltpu.SemaphoreType.DMA((4,)),
        ],
        name="load",
        cost_estimate=pl.CostEstimate(flops=0, bytes_accessed=11 << 20, transcendentals=0),
        compiler_params=PARAMS,
    )(*given, live)


def forward_kernel(start, steps, table, values, x0, x1, x3, x2, out):
    sources = (x0, x1, x2, x3)
    rows = FWD_TILES * 128
    for step in range(steps):
        total = None
        for k in range(4):
            left = []
            for r in range(FWD_TILES):
                base = (start + step * FWD_TILES + r) * 8 + 2 * k
                left.append(
                    jnp.concatenate(
                        [tile(values, table[base]), tile(values, table[base + 1])], axis=1
                    )
                )
            term = dot(jnp.concatenate(left, axis=0), sources[k][...])
            total = term if total is None else total + term
        out[step * rows : (step + 1) * rows, :] = total.astype(out.dtype)


def forward(name, start, count, dtype, table, values, sources):
    return pl.pallas_call(
        functools.partial(forward_kernel, start, count // FWD_TILES),
        out_shape=sds((count * 128, 128), dtype),
        in_specs=[SM] + [VM] * 5,
        out_specs=VM,
        name=name,
        cost_estimate=pl.CostEstimate(
            flops=2 * count * 128 * 1024 * 128, bytes_accessed=count << 15, transcendentals=0
        ),
        compiler_params=PARAMS,
    )(table, values, *sources)


def first_sum_kernel(kept, got, s1, s3, s2):
    for a, out in enumerate((s1, s2, s3)):
        total = kept[a * 1024 : a * 1024 + 1024, :] + got[a * 1024 + 1024 : a * 1024 + 2048, :].astype(F32)
        out[...] = total.astype(BF)


def first_sum(kept, got):
    return pl.pallas_call(
        first_sum_kernel,
        out_shape=(sds((1024, 128), BF),) * 3,
        in_specs=[VM] * 2,
        out_specs=(VM,) * 3,
        name="first_sum",
        compiler_params=PARAMS,
    )(kept, got)


def second_sum_kernel(own, other, g1, g3, g2, mine, s1, s3, s2):
    for b, out in enumerate((mine, s1, s2, s3)):
        part = pl.ds(b * 256, 256)
        total = own[part, :] + other[part, :].astype(F32) + g1[part, :].astype(F32)
        total = total + g2[part, :].astype(F32) + g3[part, :].astype(F32)
        out[...] = total.astype(out.dtype)


def second_sum(own, other, got):
    return pl.pallas_call(
        second_sum_kernel,
        out_shape=(sds((256, 128), F32),) + (sds((256, 128), BF),) * 3,
        in_specs=[VM] * 5,
        out_specs=(VM,) * 4,
        name="second_sum",
        compiler_params=PARAMS,
    )(own, other, *got)


def middle_kernel(own, g1, g3, g2, weight, cotangent, out, message):
    mixed = own[...] + g1[...].astype(F32) + g2[...].astype(F32) + g3[...].astype(F32)
    high, low = split(mixed)
    w = weight[...]
    summed = dot(high, w) + dot(low, w)
    gate = 1.0 / (1.0 + jnp.exp(-summed))
    out[...] = (summed * gate).astype(BF)
    slope = gate * (1.0 + summed * (1.0 - gate))
    grad = (cotangent[...].astype(F32) * slope).astype(BF)
    back = lax.dot_general(w, grad, (((1,), (1,)), ((), ())), preferred_element_type=F32)
    message[0] = back.astype(BF)
    over_rows = (((0,), (0,)), ((), ()))
    term = lax.dot_general(high, grad, over_rows, preferred_element_type=F32)
    term = term + lax.dot_general(low, grad, over_rows, preferred_element_type=F32)
    message[1], message[2] = split(term)


def middle(own, got, weight, cotangent):
    return pl.pallas_call(
        middle_kernel,
        out_shape=(sds((256, 256), BF), sds((3, 128, 256), BF)),
        in_specs=[VM] * 6,
        out_specs=(VM,) * 2,
        name="middle",
        compiler_params=PARAMS,
    )(own, *got, weight, cotangent)


def ring_sum(own, g1, g2, g3, at, terms=2):
    own, g1, g2, g3 = [joined(ref, at, terms) for ref in (own, g1, g2, g3)]
    return (own + g2) + (g1 + g3)


def gather_kernel(own, g3, g1, g2, message):
    for b, ref in enumerate((own, g1, g2, g3)):
        message[b] = ref[0]
    for n, term in enumerate(split(ring_sum(own, g1, g2, g3, 1), COL_TERMS)):
        message[4 + n] = term


def gather_step(own, got):
    return pl.pallas_call(
        gather_kernel,
        out_shape=sds((4 + COL_TERMS, 128, 256), BF),
        in_specs=[VM] * 4,
        out_specs=VM,
        name="gather_step",
        compiler_params=PARAMS,
    )(own, *got)


def backward_tiles(half, a, q, table, values, part, total):
    for b in range(4):
        base = (half * 32 + a * 8 + b * 2) * 8 + 2 * q
        upper = [tile(values, table[base]), tile(values, table[base + 1])]
        lower = [tile(values, table[base + 8]), tile(values, table[base + 9])]
        block = jnp.concatenate(
            [jnp.concatenate(upper, axis=1), jnp.concatenate(lower, axis=1)], axis=0
        )
        term = dot(part[b], block)
        total = term if total is None else total + term
    return total


def backward_kernel(half, offsets, first, table, values, *refs):
    parts, out = refs[: len(offsets)], refs[-1]
    for q in range(4):
        total = None if first else refs[len(offsets)][q]
        for a, part in zip(offsets, parts):
            total = backward_tiles(half, a, q, table, values, part, total)
        out[q] = total


BACK_COST = pl.CostEstimate(flops=1, bytes_accessed=1, transcendentals=0)


def backward(half, offsets, table, values, parts, partial):
    given = () if partial is None else (partial,)
    return pl.pallas_call(
        functools.partial(backward_kernel, half, offsets, partial is None),
        out_shape=sds((4, 128, 256), F32),
        in_specs=[SM] + [VM] * (1 + len(parts) + len(given)),
        out_specs=VM,
        name=f"backward_{half}_{offsets[0]}",
        cost_estimate=BACK_COST,
        compiler_params=PARAMS,
    )(table, values, *parts, *given)


def tie_kernel(*refs):
    del refs


def tie(values, after):
    return pl.pallas_call(
        tie_kernel,
        out_shape=[sds(value.shape, value.dtype) for value in values],
        in_specs=[AN] * (len(values) + 1),
        out_specs=[AN] * len(values),
        input_output_aliases={n: n for n in range(len(values))},
        name="tie",
        compiler_params=PARAMS,
    )(*values, after)


def last_kernel(half, offsets, table, values, p0, p3, p1, p2, o0, o3, o1, o2, partial, own, own_term, s3, s1, s2):
    sends = (s1, s2, s3)
    parts = [(o0, o1, o2, o3)[a] for a in offsets]
    term = ring_sum(p0, p1, p2, p3, 4, COL_TERMS) + ring_sum(o0, o1, o2, o3, 4, COL_TERMS)
    for n, term in enumerate(split(term, ROW_TERMS)):
        own_term[n] = term
        for out in sends:
            out[1 + n] = term
    for q in range(4):
        total = partial[q]
        for a, part in zip(offsets, parts):
            total = backward_tiles(half, a, q, table, values, part, total)
        if q == 0:
            own[...] = total
        else:
            sends[q - 1][0] = total.astype(BF)


def last(half, offsets, table, values, mine, others, partial):
    return pl.pallas_call(
        functools.partial(last_kernel, half, offsets),
        out_shape=(sds((128, 256), F32), sds((ROW_TERMS, 128, 256), BF))
        + (sds((1 + ROW_TERMS, 128, 256), BF),) * 3,
        in_specs=[SM] + [VM] * 10,
        out_specs=(VM,) * 5,
        name="backward_last",
        cost_estimate=BACK_COST,
        compiler_params=PARAMS,
    )(table, values, *mine, *others, partial)


def finish_kernel(scale, own, own_term, g3, g1, g2, grad_in, grad_weight):
    total = own[...] + g1[0].astype(F32) + g2[0].astype(F32) + g3[0].astype(F32)
    grad_in[...] = total.T.astype(BF)
    g1, g2, g3 = [joined(ref, 1, ROW_TERMS) for ref in (g1, g2, g3)]
    term = (joined(own_term, 0, ROW_TERMS) + g2) + (g1 + g3)
    grad_weight[...] = term * scale


def finish(scale, own, own_term, got):
    return pl.pallas_call(
        functools.partial(finish_kernel, scale),
        out_shape=(sds((256, 128), BF), sds((128, 256), F32)),
        in_specs=[VM] * 5,
        out_specs=(VM,) * 2,
        name="finish",
        compiler_params=PARAMS,
    )(own, own_term, *got)


def row_shift(value, k):
    return lax.ppermute(value, "row", [(i, (i + k) % 4) for i in range(4)])


def swap_cores(value):
    return lax.ppermute(value, "col", [(j, j ^ 1) for j in range(32)])


def chip_shift(value, k, x_core):
    pairs = []
    for z in range(4):
        for x in range(4):
            for core in range(2):
                if core == x_core:
                    to = (z, (x + k) % 4)
                else:
                    to = ((z + k) % 4, x)
                pairs.append(((z * 4 + x) * 2 + core, (to[0] * 4 + to[1]) * 2 + core))
    return lax.ppermute(value, "col", pairs)


ORDER = {1: (1, 3, 2), -1: (3, 1, 2)}


def shift_each(shift, values, sign, *args):
    return [shift(v, sign * k, *args) for k, v in zip(ORDER[sign], values)]


def local(features, weight, cotangent, tile_values, tile_rows, tile_cols, tile_counts):
    shifted = shift_each(row_shift, [features] * 3, 1)
    values, own_features, table = load(
        tile_values[0, 0], features, tile_rows, tile_cols, tile_counts
    )
    sources = [own_features] + shifted
    other = swap_cores(forward("forward_other", 0, 32, BF, table, values, sources))
    kept = forward("forward_sent", 40, 24, F32, table, values, sources)
    got = shift_each(chip_shift, first_sum(kept, other), 1, 0)
    kept = forward("forward_kept", 32, 8, F32, table, values, sources)
    own, *sends = second_sum(kept, other, got)
    got = shift_each(chip_shift, sends, 1, 1)
    output, message = middle(own, got, weight, cotangent)
    got = shift_each(chip_shift, [message] * 3, -1, 1)
    message = gather_step(message, got)
    first = message
    rest = shift_each(chip_shift, [message] * 3, -1, 0)
    other_first = swap_cores(first)
    partial = backward(1, (0,), table, values, (first,), None)
    partial = backward(0, (0,), table, values, (other_first,), partial)
    rest = tie(rest, partial)
    other_rest = [swap_cores(v) for v in rest]
    partial = backward(1, ORDER[-1], table, values, rest, partial)
    mine, others = (first, *rest), (other_first, *other_rest)
    own, own_term, *sends = last(0, ORDER[-1], table, values, mine, others, partial)
    got = shift_each(row_shift, sends, -1)
    grad_in, grad_weight = finish(32768.0 ** -0.5, own, own_term, got)
    return output, grad_in, grad_weight


def solution(mesh):
    placed = (
        P(("row", "col"), None),
        P(),
        P(("row", "col"), None),
        P("row", "col", None, None, None),
        P("row", "col", None),
        P("row", "col", None),
        P("row", "col"),
    )
    return jax.shard_map(
        local,
        mesh=mesh,
        in_specs=placed,
        out_specs=(P(("row", "col"), None), P(("row", "col"), None), P()),
        check_vma=False,
    )
```

```python
import functools

import jax
import jax.numpy as jnp
from jax import lax
from jax.experimental import pallas as pl
from jax.experimental.pallas import tpu as pltpu
from jax.sharding import PartitionSpec as P

BF = jnp.bfloat16
F32 = jnp.float32
VM = pl.BlockSpec(memory_space=pltpu.VMEM)
SM = pl.BlockSpec(memory_space=pltpu.SMEM)
HB = pl.BlockSpec(memory_space=pltpu.HBM)
AN = pl.BlockSpec(memory_space=pl.ANY)
PARAMS = pltpu.CompilerParams(vmem_limit_bytes=24 << 20)

FWD_TILES = 4
COL_TERMS = 1
ROW_TERMS = 1


def sds(shape, dtype):
    return jax.ShapeDtypeStruct(shape, dtype)


def dot(a, b):
    return jnp.dot(a, b, preferred_element_type=F32)


def split(v, terms=2):
    high = v.astype(BF)
    if terms == 1:
        return (high,)
    return high, (v - high.astype(F32)).astype(BF)


def joined(ref, at, terms=2):
    high = ref[at].astype(F32)
    return high if terms == 1 else high + ref[at + 1].astype(F32)


def tile(values, slot):
    found = values[jnp.maximum(slot, 0)]
    return jnp.where(slot >= 0, found, jnp.zeros_like(found))


def load_kernel(values, features, rows_in, cols_in, live, held, own, table, slot_rows, slot_cols, sem):
    pairs = ((rows_in, slot_rows), (cols_in, slot_cols))
    small = [pltpu.make_async_copy(*pair, sem.at[2 + n]) for n, pair in enumerate(pairs)]
    copies = [
        pltpu.make_async_copy(values, held, sem.at[0]),
        pltpu.make_async_copy(features, own, sem.at[1]),
    ]
    for copy in small + copies:
        copy.start()
    row, col = lax.axis_index("row"), lax.axis_index("col")
    core, x, z = col & 1, (col >> 1) & 3, col >> 3

    def clear(step, carry):
        for u in range(16):
            table[step * 16 + u] = -1
        return carry

    lax.fori_loop(0, 32, clear, 0)
    for copy in small:
        copy.wait()

    def place(slot):
        tile_row, tile_col = slot_rows[0, 0, slot], slot_cols[0, 0, slot]
        parity = (tile_row >> 1) & 1
        dx = ((tile_row >> 2) - x) & 3
        dz = ((tile_row >> 4) - z) & 3
        a = jnp.where(parity == 0, dx, dz)
        b = jnp.where(parity == 0, dz, dx)
        half = 1 - (parity ^ core)
        source = ((row - (tile_col >> 1)) & 3) * 2 + (tile_col & 1)
        table[(half * 32 + a * 8 + b * 2 + (tile_row & 1)) * 8 + source] = slot

    count = live[0, 0]

    def place_four(step, carry):
        for u in range(4):
            place(step * 4 + u)
        return carry

    def place_one(slot, carry):
        place(slot)
        return carry

    lax.fori_loop(0, count >> 2, place_four, 0)
    lax.fori_loop((count >> 2) << 2, count, place_one, 0)
    for copy in copies:
        copy.wait()


def load(values, features, slot_rows, slot_cols, live):
    given = (values, features, slot_rows, slot_cols)
    given = [pltpu.with_memory_space_constraint(value, pltpu.HBM) for value in given]
    slots = values.shape[0]
    return pl.pallas_call(
        load_kernel,
        out_shape=(sds(values.shape, BF), sds(features.shape, BF), pltpu.SMEM((512,), jnp.int32)),
        in_specs=[HB] * 4 + [SM],
        out_specs=(VM, VM, SM),
        scratch_shapes=[
            pltpu.SMEM((1, 1, slots), jnp.int32),
            pltpu.SMEM((1, 1, slots), jnp.int32),
            pltpu.SemaphoreType.DMA((4,)),
        ],
        name="load",
        cost_estimate=pl.CostEstimate(flops=0, bytes_accessed=11 << 20, transcendentals=0),
        compiler_params=PARAMS,
    )(*given, live)


def forward_kernel(start, steps, table, values, x0, x1, x3, x2, *refs):
    out = refs[-1]
    sources = (x0, x1, x2, x3)
    rows = FWD_TILES * 128
    for step in range(steps):
        total = None
        for k in range(4):
            left = []
            for r in range(FWD_TILES):
                base = (start + step * FWD_TILES + r) * 8 + 2 * k
                left.append(
                    jnp.concatenate(
                        [tile(values, table[base]), tile(values, table[base + 1])], axis=1
                    )
                )
            term = dot(jnp.concatenate(left, axis=0), sources[k][...])
            total = term if total is None else total + term
        out[step * rows : (step + 1) * rows, :] = total.astype(out.dtype)


def forward(name, start, count, dtype, table, values, sources, *after):
    return pl.pallas_call(
        functools.partial(forward_kernel, start, count // FWD_TILES),
        out_shape=sds((count * 128, 128), dtype),
        in_specs=[SM] + [VM] * 5 + [AN] * len(after),
        out_specs=VM,
        name=name,
        cost_estimate=pl.CostEstimate(
            flops=2 * count * 128 * 1024 * 128, bytes_accessed=count << 15, transcendentals=0
        ),
        compiler_params=PARAMS,
    )(table, values, *sources, *after)


def first_sum_kernel(kept, got, s1, s3, s2):
    for a, out in enumerate((s1, s2, s3)):
        total = kept[a * 1024 : a * 1024 + 1024, :] + got[a * 1024 : a * 1024 + 1024, :].astype(F32)
        out[...] = total.astype(BF)


def first_sum(kept, got):
    return pl.pallas_call(
        first_sum_kernel,
        out_shape=(sds((1024, 128), BF),) * 3,
        in_specs=[VM] * 2,
        out_specs=(VM,) * 3,
        name="first_sum",
        compiler_params=PARAMS,
    )(kept, got)


def second_sum_kernel(own, other, g1, g3, g2, mine, s1, s3, s2):
    for b, out in enumerate((mine, s1, s2, s3)):
        part = pl.ds(b * 256, 256)
        total = own[part, :] + other[part, :].astype(F32) + g1[part, :].astype(F32)
        total = total + g2[part, :].astype(F32) + g3[part, :].astype(F32)
        out[...] = total.astype(out.dtype)


def second_sum(own, other, got):
    return pl.pallas_call(
        second_sum_kernel,
        out_shape=(sds((256, 128), F32),) + (sds((256, 128), BF),) * 3,
        in_specs=[VM] * 5,
        out_specs=(VM,) * 4,
        name="second_sum",
        compiler_params=PARAMS,
    )(own, other, *got)


def middle_kernel(own, g1, g3, g2, weight, cotangent, out, message):
    mixed = own[...] + g1[...].astype(F32) + g2[...].astype(F32) + g3[...].astype(F32)
    high, low = split(mixed)
    w = weight[...]
    summed = dot(high, w) + dot(low, w)
    gate = 1.0 / (1.0 + jnp.exp(-summed))
    out[...] = (summed * gate).astype(BF)
    slope = gate * (1.0 + summed * (1.0 - gate))
    grad = (cotangent[...].astype(F32) * slope).astype(BF)
    back = lax.dot_general(w, grad, (((1,), (1,)), ((), ())), preferred_element_type=F32)
    message[0] = back.astype(BF)
    over_rows = (((0,), (0,)), ((), ()))
    term = lax.dot_general(high, grad, over_rows, preferred_element_type=F32)
    term = term + lax.dot_general(low, grad, over_rows, preferred_element_type=F32)
    message[1], message[2] = split(term)


def middle(own, got, weight, cotangent):
    return pl.pallas_call(
        middle_kernel,
        out_shape=(sds((256, 256), BF), sds((3, 128, 256), BF)),
        in_specs=[VM] * 6,
        out_specs=(VM,) * 2,
        name="middle",
        compiler_params=PARAMS,
    )(own, *got, weight, cotangent)


def ring_sum(own, g1, g2, g3, at, terms=2):
    own, g1, g2, g3 = [joined(ref, at, terms) for ref in (own, g1, g2, g3)]
    return (own + g2) + (g1 + g3)


def gather_kernel(own, g3, g1, g2, message):
    for b, ref in enumerate((own, g1, g2, g3)):
        message[b] = ref[0]
    for n, term in enumerate(split(ring_sum(own, g1, g2, g3, 1), COL_TERMS)):
        message[4 + n] = term


def gather_step(own, got):
    return pl.pallas_call(
        gather_kernel,
        out_shape=sds((4 + COL_TERMS, 128, 256), BF),
        in_specs=[VM] * 4,
        out_specs=VM,
        name="gather_step",
        compiler_params=PARAMS,
    )(own, *got)


def backward_tiles(half, a, q, table, values, part, total):
    for b in range(4):
        base = (half * 32 + a * 8 + b * 2) * 8 + 2 * q
        upper = [tile(values, table[base]), tile(values, table[base + 1])]
        lower = [tile(values, table[base + 8]), tile(values, table[base + 9])]
        block = jnp.concatenate(
            [jnp.concatenate(upper, axis=1), jnp.concatenate(lower, axis=1)], axis=0
        )
        term = dot(part[b], block)
        total = term if total is None else total + term
    return total


def backward_kernel(half, offsets, first, table, values, *refs):
    parts, out = refs[: len(offsets)], refs[-1]
    for q in range(4):
        total = None if first else refs[len(offsets)][q]
        for a, part in zip(offsets, parts):
            total = backward_tiles(half, a, q, table, values, part, total)
        out[q] = total


BACK_COST = pl.CostEstimate(flops=1, bytes_accessed=1, transcendentals=0)


def backward(half, offsets, table, values, parts, partial):
    given = () if partial is None else (partial,)
    return pl.pallas_call(
        functools.partial(backward_kernel, half, offsets, partial is None),
        out_shape=sds((4, 128, 256), F32),
        in_specs=[SM] + [VM] * (1 + len(parts) + len(given)),
        out_specs=VM,
        name=f"backward_{half}_{offsets[0]}",
        cost_estimate=BACK_COST,
        compiler_params=PARAMS,
    )(table, values, *parts, *given)


def tie_kernel(*refs):
    del refs


def tie(values, after):
    return pl.pallas_call(
        tie_kernel,
        out_shape=[sds(value.shape, value.dtype) for value in values],
        in_specs=[AN] * (len(values) + 1),
        out_specs=[AN] * len(values),
        input_output_aliases={n: n for n in range(len(values))},
        name="tie",
        compiler_params=PARAMS,
    )(*values, after)


def last_kernel(half, offsets, table, values, p0, p3, p1, p2, o0, o3, o1, o2, partial, own, own_term, s3, s1, s2):
    sends = (s1, s2, s3)
    parts = [(o0, o1, o2, o3)[a] for a in offsets]
    term = ring_sum(p0, p1, p2, p3, 4, COL_TERMS) + ring_sum(o0, o1, o2, o3, 4, COL_TERMS)
    for n, term in enumerate(split(term, ROW_TERMS)):
        own_term[n] = term
        for out in sends:
            out[1 + n] = term
    for q in range(4):
        total = partial[q]
        for a, part in zip(offsets, parts):
            total = backward_tiles(half, a, q, table, values, part, total)
        if q == 0:
            own[...] = total
        else:
            sends[q - 1][0] = total.astype(BF)


def last(half, offsets, table, values, mine, others, partial):
    return pl.pallas_call(
        functools.partial(last_kernel, half, offsets),
        out_shape=(sds((128, 256), F32), sds((ROW_TERMS, 128, 256), BF))
        + (sds((1 + ROW_TERMS, 128, 256), BF),) * 3,
        in_specs=[SM] + [VM] * 10,
        out_specs=(VM,) * 5,
        name="backward_last",
        cost_estimate=BACK_COST,
        compiler_params=PARAMS,
    )(table, values, *mine, *others, partial)


def finish_kernel(scale, own, own_term, g3, g1, g2, grad_in, grad_weight):
    total = own[...] + g1[0].astype(F32) + g2[0].astype(F32) + g3[0].astype(F32)
    grad_in[...] = total.T.astype(BF)
    g1, g2, g3 = [joined(ref, 1, ROW_TERMS) for ref in (g1, g2, g3)]
    term = (joined(own_term, 0, ROW_TERMS) + g2) + (g1 + g3)
    grad_weight[...] = term * scale


def finish(scale, own, own_term, got):
    return pl.pallas_call(
        functools.partial(finish_kernel, scale),
        out_shape=(sds((256, 128), BF), sds((128, 256), F32)),
        in_specs=[VM] * 5,
        out_specs=(VM,) * 2,
        name="finish",
        compiler_params=PARAMS,
    )(own, own_term, *got)


def row_shift(value, k):
    return lax.ppermute(value, "row", [(i, (i + k) % 4) for i in range(4)])


def swap_cores(value):
    return lax.ppermute(value, "col", [(j, j ^ 1) for j in range(32)])


def chip_shift(value, k, x_core):
    pairs = []
    for z in range(4):
        for x in range(4):
            for core in range(2):
                if core == x_core:
                    to = (z, (x + k) % 4)
                else:
                    to = ((z + k) % 4, x)
                pairs.append(((z * 4 + x) * 2 + core, (to[0] * 4 + to[1]) * 2 + core))
    return lax.ppermute(value, "col", pairs)


ORDER = {1: (1, 3, 2), -1: (3, 1, 2)}


def shift_each(shift, values, sign, *args):
    return [shift(v, sign * k, *args) for k, v in zip(ORDER[sign], values)]


def local(features, weight, cotangent, tile_values, tile_rows, tile_cols, tile_counts):
    shifted = shift_each(row_shift, [features] * 3, 1)
    values, own_features, table = load(
        tile_values[0, 0], features, tile_rows, tile_cols, tile_counts
    )
    sources = [own_features] + shifted
    other = swap_cores(forward("forward_other", 8, 24, BF, table, values, sources))
    sent = forward("forward_sent", 40, 24, F32, table, values, sources)
    got = shift_each(chip_shift, first_sum(sent, other), 1, 0)
    other = swap_cores(forward("forward_rest", 0, 8, BF, table, values, sources, sent))
    kept = forward("forward_kept", 32, 8, F32, table, values, sources)
    own, *sends = second_sum(kept, other, got)
    got = shift_each(chip_shift, sends, 1, 1)
    output, message = middle(own, got, weight, cotangent)
    got = shift_each(chip_shift, [message] * 3, -1, 1)
    message = gather_step(message, got)
    first = message
    rest = shift_each(chip_shift, [message] * 3, -1, 0)
    other_first = swap_cores(first)
    partial = backward(1, (0,), table, values, (first,), None)
    partial = backward(0, (0,), table, values, (other_first,), partial)
    rest = tie(rest, partial)
    other_rest = [swap_cores(v) for v in rest]
    partial = backward(1, ORDER[-1], table, values, rest, partial)
    mine, others = (first, *rest), (other_first, *other_rest)
    own, own_term, *sends = last(0, ORDER[-1], table, values, mine, others, partial)
    got = shift_each(row_shift, sends, -1)
    grad_in, grad_weight = finish(32768.0 ** -0.5, own, own_term, got)
    return output, grad_in, grad_weight


def solution(mesh):
    placed = (
        P(("row", "col"), None),
        P(),
        P(("row", "col"), None),
        P("row", "col", None, None, None),
        P("row", "col", None),
        P("row", "col", None),
        P("row", "col"),
    )
    return jax.shard_map(
        local,
        mesh=mesh,
        in_specs=placed,
        out_specs=(P(("row", "col"), None), P(("row", "col"), None), P()),
        check_vma=False,
    )
```

```python
import functools

import jax
import jax.numpy as jnp
from jax import lax
from jax.experimental import pallas as pl
from jax.experimental.pallas import tpu as pltpu
from jax.sharding import PartitionSpec as P

BF = jnp.bfloat16
F32 = jnp.float32
VM = pl.BlockSpec(memory_space=pltpu.VMEM)
SM = pl.BlockSpec(memory_space=pltpu.SMEM)
HB = pl.BlockSpec(memory_space=pltpu.HBM)
AN = pl.BlockSpec(memory_space=pl.ANY)
PARAMS = pltpu.CompilerParams(vmem_limit_bytes=24 << 20)

FWD_TILES = 4
COL_TERMS = 1
ROW_TERMS = 1


def sds(shape, dtype):
    return jax.ShapeDtypeStruct(shape, dtype)


def dot(a, b):
    return jnp.dot(a, b, preferred_element_type=F32)


def split(v, terms=2):
    high = v.astype(BF)
    if terms == 1:
        return (high,)
    return high, (v - high.astype(F32)).astype(BF)


def joined(ref, at, terms=2):
    high = ref[at].astype(F32)
    return high if terms == 1 else high + ref[at + 1].astype(F32)


def tile(values, slot):
    found = values[jnp.maximum(slot, 0)]
    return jnp.where(slot >= 0, found, jnp.zeros_like(found))


def load_kernel(values, features, rows_in, cols_in, live, held, own, table, slot_rows, slot_cols, sem):
    pairs = ((rows_in, slot_rows), (cols_in, slot_cols))
    small = [pltpu.make_async_copy(*pair, sem.at[2 + n]) for n, pair in enumerate(pairs)]
    copies = [
        pltpu.make_async_copy(values, held, sem.at[0]),
        pltpu.make_async_copy(features, own, sem.at[1]),
    ]
    for copy in small + copies:
        copy.start()
    row, col = lax.axis_index("row"), lax.axis_index("col")
    core, x, z = col & 1, (col >> 1) & 3, col >> 3

    def clear(step, carry):
        for u in range(16):
            table[step * 16 + u] = -1
        return carry

    lax.fori_loop(0, 32, clear, 0)
    for copy in small:
        copy.wait()

    def place(slot):
        tile_row, tile_col = slot_rows[0, 0, slot], slot_cols[0, 0, slot]
        parity = (tile_row >> 1) & 1
        dx = ((tile_row >> 2) - x) & 3
        dz = ((tile_row >> 4) - z) & 3
        a = jnp.where(parity == 0, dx, dz)
        b = jnp.where(parity == 0, dz, dx)
        half = 1 - (parity ^ core)
        source = ((row - (tile_col >> 1)) & 3) * 2 + (tile_col & 1)
        table[(half * 32 + a * 8 + b * 2 + (tile_row & 1)) * 8 + source] = slot

    count = live[0, 0]

    def place_four(step, carry):
        for u in range(4):
            place(step * 4 + u)
        return carry

    def place_one(slot, carry):
        place(slot)
        return carry

    lax.fori_loop(0, count >> 2, place_four, 0)
    lax.fori_loop((count >> 2) << 2, count, place_one, 0)
    for copy in copies:
        copy.wait()


def load(values, features, slot_rows, slot_cols, live):
    given = (values, features, slot_rows, slot_cols)
    given = [pltpu.with_memory_space_constraint(value, pltpu.HBM) for value in given]
    slots = values.shape[0]
    return pl.pallas_call(
        load_kernel,
        out_shape=(sds(values.shape, BF), sds(features.shape, BF), pltpu.SMEM((512,), jnp.int32)),
        in_specs=[HB] * 4 + [SM],
        out_specs=(VM, VM, SM),
        scratch_shapes=[
            pltpu.SMEM((1, 1, slots), jnp.int32),
            pltpu.SMEM((1, 1, slots), jnp.int32),
            pltpu.SemaphoreType.DMA((4,)),
        ],
        name="load",
        cost_estimate=pl.CostEstimate(flops=0, bytes_accessed=11 << 20, transcendentals=0),
        compiler_params=PARAMS,
    )(*given, live)


def forward_kernel(start, steps, table, values, x0, x1, x3, x2, *refs):
    out = refs[-1]
    sources = (x0, x1, x2, x3)
    rows = FWD_TILES * 128
    for step in range(steps):
        total = None
        for k in range(4):
            left = []
            for r in range(FWD_TILES):
                base = (start + step * FWD_TILES + r) * 8 + 2 * k
                left.append(
                    jnp.concatenate(
                        [tile(values, table[base]), tile(values, table[base + 1])], axis=1
                    )
                )
            term = dot(jnp.concatenate(left, axis=0), sources[k][...])
            total = term if total is None else total + term
        out[step * rows : (step + 1) * rows, :] = total.astype(out.dtype)


def forward(name, start, count, dtype, table, values, sources, *after):
    return pl.pallas_call(
        functools.partial(forward_kernel, start, count // FWD_TILES),
        out_shape=sds((count * 128, 128), dtype),
        in_specs=[SM] + [VM] * 5 + [AN] * len(after),
        out_specs=VM,
        name=name,
        cost_estimate=pl.CostEstimate(
            flops=2 * count * 128 * 1024 * 128, bytes_accessed=count << 15, transcendentals=0
        ),
        compiler_params=PARAMS,
    )(table, values, *sources, *after)


def first_sum_kernel(kept, got, s1, s3, s2):
    for a, out in enumerate((s1, s2, s3)):
        total = kept[a * 1024 : a * 1024 + 1024, :] + got[a * 1024 : a * 1024 + 1024, :].astype(F32)
        out[...] = total.astype(BF)


def first_sum(kept, got):
    return pl.pallas_call(
        first_sum_kernel,
        out_shape=(sds((1024, 128), BF),) * 3,
        in_specs=[VM] * 2,
        out_specs=(VM,) * 3,
        name="first_sum",
        compiler_params=PARAMS,
    )(kept, got)


def second_sum_kernel(own, other, g1, g3, g2, mine, s1, s3, s2):
    for b, out in enumerate((mine, s1, s2, s3)):
        part = pl.ds(b * 256, 256)
        total = own[part, :] + other[part, :].astype(F32) + g1[part, :].astype(F32)
        total = total + g2[part, :].astype(F32) + g3[part, :].astype(F32)
        out[...] = total.astype(out.dtype)


def second_sum(own, other, got):
    return pl.pallas_call(
        second_sum_kernel,
        out_shape=(sds((256, 128), F32),) + (sds((256, 128), BF),) * 3,
        in_specs=[VM] * 5,
        out_specs=(VM,) * 4,
        name="second_sum",
        compiler_params=PARAMS,
    )(own, other, *got)


def middle_kernel(own, g1, g3, g2, weight, cotangent, out, message):
    mixed = own[...] + g1[...].astype(F32) + g2[...].astype(F32) + g3[...].astype(F32)
    high, low = split(mixed)
    w = weight[...]
    summed = dot(high, w) + dot(low, w)
    gate = 1.0 / (1.0 + jnp.exp(-summed))
    out[...] = summed * gate
    slope = gate * (1.0 + summed * (1.0 - gate))
    grad = (cotangent[...].astype(F32) * slope).astype(BF)
    back = lax.dot_general(w, grad, (((1,), (1,)), ((), ())), preferred_element_type=F32)
    message[0] = back.astype(BF)
    over_rows = (((0,), (0,)), ((), ()))
    term = lax.dot_general(high, grad, over_rows, preferred_element_type=F32)
    term = term + lax.dot_general(low, grad, over_rows, preferred_element_type=F32)
    message[1], message[2] = split(term)


def middle(own, got, weight, cotangent):
    return pl.pallas_call(
        middle_kernel,
        out_shape=(sds((256, 256), F32), sds((3, 128, 256), BF)),
        in_specs=[VM] * 6,
        out_specs=(VM,) * 2,
        name="middle",
        compiler_params=PARAMS,
    )(own, *got, weight, cotangent)


def ring_sum(own, g1, g2, g3, at, terms=2):
    own, g1, g2, g3 = [joined(ref, at, terms) for ref in (own, g1, g2, g3)]
    return (own + g2) + (g1 + g3)


def gather_kernel(own, g3, g1, g2, message):
    for b, ref in enumerate((own, g1, g2, g3)):
        message[b] = ref[0]
    for n, term in enumerate(split(ring_sum(own, g1, g2, g3, 1), COL_TERMS)):
        message[4 + n] = term


def gather_step(own, got):
    return pl.pallas_call(
        gather_kernel,
        out_shape=sds((4 + COL_TERMS, 128, 256), BF),
        in_specs=[VM] * 4,
        out_specs=VM,
        name="gather_step",
        compiler_params=PARAMS,
    )(own, *got)


def backward_tiles(half, a, q, table, values, part, total):
    for b in range(4):
        base = (half * 32 + a * 8 + b * 2) * 8 + 2 * q
        upper = [tile(values, table[base]), tile(values, table[base + 1])]
        lower = [tile(values, table[base + 8]), tile(values, table[base + 9])]
        block = jnp.concatenate(
            [jnp.concatenate(upper, axis=1), jnp.concatenate(lower, axis=1)], axis=0
        )
        term = dot(part[b], block)
        total = term if total is None else total + term
    return total


def backward_kernel(half, offsets, first, table, values, *refs):
    parts, out = refs[: len(offsets)], refs[-1]
    for q in range(4):
        total = None if first else refs[len(offsets)][q]
        for a, part in zip(offsets, parts):
            total = backward_tiles(half, a, q, table, values, part, total)
        out[q] = total


BACK_COST = pl.CostEstimate(flops=1, bytes_accessed=1, transcendentals=0)


def backward(half, offsets, table, values, parts, partial):
    given = () if partial is None else (partial,)
    return pl.pallas_call(
        functools.partial(backward_kernel, half, offsets, partial is None),
        out_shape=sds((4, 128, 256), F32),
        in_specs=[SM] + [VM] * (1 + len(parts) + len(given)),
        out_specs=VM,
        name=f"backward_{half}_{offsets[0]}",
        cost_estimate=BACK_COST,
        compiler_params=PARAMS,
    )(table, values, *parts, *given)


def backward_first_kernel(table, values, part, active, out, output):
    for q in range(4):
        out[q] = backward_tiles(1, 0, q, table, values, part, None)
    output[...] = active[...].astype(BF)


def backward_first(table, values, part, active):
    return pl.pallas_call(
        backward_first_kernel,
        out_shape=(sds((4, 128, 256), F32), sds(active.shape, BF)),
        in_specs=[SM] + [VM] * 3,
        out_specs=(VM,) * 2,
        name="backward_first",
        cost_estimate=BACK_COST,
        compiler_params=PARAMS,
    )(table, values, part, active)


def tie_kernel(*refs):
    del refs


def tie(values, after):
    return pl.pallas_call(
        tie_kernel,
        out_shape=[sds(value.shape, value.dtype) for value in values],
        in_specs=[AN] * (len(values) + 1),
        out_specs=[AN] * len(values),
        input_output_aliases={n: n for n in range(len(values))},
        name="tie",
        compiler_params=PARAMS,
    )(*values, after)


def last_kernel(half, offsets, table, values, p0, p3, p1, p2, o0, o3, o1, o2, partial, own_term, s3, s1, s2):
    sends = (s1, s2, s3)
    parts = [(o0, o1, o2, o3)[a] for a in offsets]
    term = ring_sum(p0, p1, p2, p3, 4, COL_TERMS) + ring_sum(o0, o1, o2, o3, 4, COL_TERMS)
    for n, term in enumerate(split(term, ROW_TERMS)):
        own_term[n] = term
        for out in sends:
            out[1 + n] = term
    for q in range(1, 4):
        total = partial[q]
        for a, part in zip(offsets, parts):
            total = backward_tiles(half, a, q, table, values, part, total)
        sends[q - 1][0] = total.astype(BF)


def last(half, offsets, table, values, mine, others, partial):
    return pl.pallas_call(
        functools.partial(last_kernel, half, offsets),
        out_shape=(sds((ROW_TERMS, 128, 256), BF),) + (sds((1 + ROW_TERMS, 128, 256), BF),) * 3,
        in_specs=[SM] + [VM] * 10,
        out_specs=(VM,) * 4,
        name="backward_last",
        cost_estimate=BACK_COST,
        compiler_params=PARAMS,
    )(table, values, *mine, *others, partial)


def kept_kernel(half, offsets, table, values, r1, r2, r3, partial, after, own):
    del after
    total = partial[0]
    for a, part in zip(offsets, (r1, r2, r3)):
        total = backward_tiles(half, a, 0, table, values, part, total)
    own[...] = total


def kept_quarter(half, offsets, table, values, rest, partial, after):
    return pl.pallas_call(
        functools.partial(kept_kernel, half, offsets),
        out_shape=sds((128, 256), F32),
        in_specs=[SM] + [VM] * 5 + [AN],
        out_specs=VM,
        name="backward_kept",
        cost_estimate=BACK_COST,
        compiler_params=PARAMS,
    )(table, values, *rest, partial, after)


def finish_kernel(scale, own, own_term, g3, g1, g2, grad_in, grad_weight):
    total = own[...] + g1[0].astype(F32) + g2[0].astype(F32) + g3[0].astype(F32)
    grad_in[...] = total.T.astype(BF)
    g1, g2, g3 = [joined(ref, 1, ROW_TERMS) for ref in (g1, g2, g3)]
    term = (joined(own_term, 0, ROW_TERMS) + g2) + (g1 + g3)
    grad_weight[...] = term * scale


def finish(scale, own, own_term, got):
    return pl.pallas_call(
        functools.partial(finish_kernel, scale),
        out_shape=(sds((256, 128), BF), sds((128, 256), F32)),
        in_specs=[VM] * 5,
        out_specs=(VM,) * 2,
        name="finish",
        compiler_params=PARAMS,
    )(own, own_term, *got)


def row_shift(value, k):
    return lax.ppermute(value, "row", [(i, (i + k) % 4) for i in range(4)])


def swap_cores(value):
    return lax.ppermute(value, "col", [(j, j ^ 1) for j in range(32)])


def chip_shift(value, k, x_core):
    pairs = []
    for z in range(4):
        for x in range(4):
            for core in range(2):
                if core == x_core:
                    to = (z, (x + k) % 4)
                else:
                    to = ((z + k) % 4, x)
                pairs.append(((z * 4 + x) * 2 + core, (to[0] * 4 + to[1]) * 2 + core))
    return lax.ppermute(value, "col", pairs)


ORDER = {1: (1, 3, 2), -1: (3, 1, 2)}


def shift_each(shift, values, sign, *args):
    return [shift(v, sign * k, *args) for k, v in zip(ORDER[sign], values)]


def local(features, weight, cotangent, tile_values, tile_rows, tile_cols, tile_counts):
    shifted = shift_each(row_shift, [features] * 3, 1)
    values, own_features, table = load(
        tile_values[0, 0], features, tile_rows, tile_cols, tile_counts
    )
    sources = [own_features] + shifted
    other = swap_cores(forward("forward_other", 8, 24, BF, table, values, sources))
    sent = forward("forward_sent", 40, 24, F32, table, values, sources)
    got = shift_each(chip_shift, first_sum(sent, other), 1, 0)
    other = swap_cores(forward("forward_rest", 0, 8, BF, table, values, sources, sent))
    kept = forward("forward_kept", 32, 8, F32, table, values, sources)
    own, *sends = second_sum(kept, other, got)
    got = shift_each(chip_shift, sends, 1, 1)
    active, message = middle(own, got, weight, cotangent)
    got = shift_each(chip_shift, [message] * 3, -1, 1)
    message = gather_step(message, got)
    first = message
    rest = shift_each(chip_shift, [message] * 3, -1, 0)
    other_first = swap_cores(first)
    partial, output = backward_first(table, values, first, active)
    partial = backward(0, (0,), table, values, (other_first,), partial)
    rest = tie(rest, partial)
    other_rest = [swap_cores(v) for v in rest]
    partial = backward(1, ORDER[-1], table, values, rest, partial)
    mine, others = (first, *rest), (other_first, *other_rest)
    own_term, *sends = last(0, ORDER[-1], table, values, mine, others, partial)
    own = kept_quarter(0, ORDER[-1], table, values, other_rest, partial, own_term)
    got = shift_each(row_shift, sends, -1)
    grad_in, grad_weight = finish(32768.0 ** -0.5, own, own_term, got)
    return output, grad_in, grad_weight


def solution(mesh):
    placed = (
        P(("row", "col"), None),
        P(),
        P(("row", "col"), None),
        P("row", "col", None, None, None),
        P("row", "col", None),
        P("row", "col", None),
        P("row", "col"),
    )
    return jax.shard_map(
        local,
        mesh=mesh,
        in_specs=placed,
        out_specs=(P(("row", "col"), None), P(("row", "col"), None), P()),
        check_vma=False,
    )
```

```python
import functools

import jax
import jax.numpy as jnp
from jax import lax
from jax.experimental import pallas as pl
from jax.experimental.pallas import tpu as pltpu
from jax.sharding import PartitionSpec as P

BF = jnp.bfloat16
F32 = jnp.float32
VM = pl.BlockSpec(memory_space=pltpu.VMEM)
SM = pl.BlockSpec(memory_space=pltpu.SMEM)
HB = pl.BlockSpec(memory_space=pltpu.HBM)
AN = pl.BlockSpec(memory_space=pl.ANY)
PARAMS = pltpu.CompilerParams(vmem_limit_bytes=24 << 20)

FWD_TILES = 4
COL_TERMS = 1
ROW_TERMS = 1


def sds(shape, dtype):
    return jax.ShapeDtypeStruct(shape, dtype)


def dot(a, b):
    return jnp.dot(a, b, preferred_element_type=F32)


def split(v, terms=2):
    high = v.astype(BF)
    if terms == 1:
        return (high,)
    return high, (v - high.astype(F32)).astype(BF)


def joined(ref, at, terms=2):
    high = ref[at].astype(F32)
    return high if terms == 1 else high + ref[at + 1].astype(F32)


def tile(values, slot):
    found = values[jnp.maximum(slot, 0)]
    return jnp.where(slot >= 0, found, jnp.zeros_like(found))


def load_kernel(values, features, rows_in, cols_in, live, held, own, table, slot_rows, slot_cols, sem):
    pairs = ((rows_in, slot_rows), (cols_in, slot_cols))
    small = [pltpu.make_async_copy(*pair, sem.at[2 + n]) for n, pair in enumerate(pairs)]
    copies = [
        pltpu.make_async_copy(values, held, sem.at[0]),
        pltpu.make_async_copy(features, own, sem.at[1]),
    ]
    for copy in small + copies:
        copy.start()
    row, col = lax.axis_index("row"), lax.axis_index("col")
    core, x, z = col & 1, (col >> 1) & 3, col >> 3

    def clear(step, carry):
        for u in range(16):
            table[step * 16 + u] = -1
        return carry

    lax.fori_loop(0, 32, clear, 0)
    for copy in small:
        copy.wait()

    def place(slot):
        tile_row, tile_col = slot_rows[0, 0, slot], slot_cols[0, 0, slot]
        parity = (tile_row >> 1) & 1
        dx = ((tile_row >> 2) - x) & 3
        dz = ((tile_row >> 4) - z) & 3
        a = jnp.where(parity == 0, dx, dz)
        b = jnp.where(parity == 0, dz, dx)
        half = 1 - (parity ^ core)
        source = ((row - (tile_col >> 1)) & 3) * 2 + (tile_col & 1)
        table[(half * 32 + a * 8 + b * 2 + (tile_row & 1)) * 8 + source] = slot

    count = live[0, 0]

    def place_four(step, carry):
        for u in range(4):
            place(step * 4 + u)
        return carry

    def place_one(slot, carry):
        place(slot)
        return carry

    lax.fori_loop(0, count >> 2, place_four, 0)
    lax.fori_loop((count >> 2) << 2, count, place_one, 0)
    for copy in copies:
        copy.wait()


def load(values, features, slot_rows, slot_cols, live):
    given = (values, features, slot_rows, slot_cols)
    given = [pltpu.with_memory_space_constraint(value, pltpu.HBM) for value in given]
    slots = values.shape[0]
    return pl.pallas_call(
        load_kernel,
        out_shape=(sds(values.shape, BF), sds(features.shape, BF), pltpu.SMEM((512,), jnp.int32)),
        in_specs=[HB] * 4 + [SM],
        out_specs=(VM, VM, SM),
        scratch_shapes=[
            pltpu.SMEM((1, 1, slots), jnp.int32),
            pltpu.SMEM((1, 1, slots), jnp.int32),
            pltpu.SemaphoreType.DMA((4,)),
        ],
        name="load",
        cost_estimate=pl.CostEstimate(flops=0, bytes_accessed=11 << 20, transcendentals=0),
        compiler_params=PARAMS,
    )(*given, live)


def forward_kernel(start, steps, table, values, x0, x1, x3, x2, *refs):
    out = refs[-1]
    sources = (x0, x1, x2, x3)
    rows = FWD_TILES * 128
    for step in range(steps):
        total = None
        for k in range(4):
            left = []
            for r in range(FWD_TILES):
                base = (start + step * FWD_TILES + r) * 8 + 2 * k
                left.append(
                    jnp.concatenate(
                        [tile(values, table[base]), tile(values, table[base + 1])], axis=1
                    )
                )
            term = dot(jnp.concatenate(left, axis=0), sources[k][...])
            total = term if total is None else total + term
        out[step * rows : (step + 1) * rows, :] = total.astype(out.dtype)


def forward(name, start, count, dtype, table, values, sources, *after):
    return pl.pallas_call(
        functools.partial(forward_kernel, start, count // FWD_TILES),
        out_shape=sds((count * 128, 128), dtype),
        in_specs=[SM] + [VM] * 5 + [AN] * len(after),
        out_specs=VM,
        name=name,
        cost_estimate=pl.CostEstimate(
            flops=2 * count * 128 * 1024 * 128, bytes_accessed=count << 15, transcendentals=0
        ),
        compiler_params=PARAMS,
    )(table, values, *sources, *after)


def first_sum_kernel(kept, got, s1, s3, s2):
    for a, out in enumerate((s1, s2, s3)):
        total = kept[a * 1024 : a * 1024 + 1024, :] + got[a * 1024 : a * 1024 + 1024, :].astype(F32)
        out[...] = total.astype(BF)


def first_sum(kept, got):
    return pl.pallas_call(
        first_sum_kernel,
        out_shape=(sds((1024, 128), BF),) * 3,
        in_specs=[VM] * 2,
        out_specs=(VM,) * 3,
        name="first_sum",
        compiler_params=PARAMS,
    )(kept, got)


def second_sum_kernel(own, other, g1, g3, g2, mine, s1, s3, s2):
    for b, out in enumerate((mine, s1, s2, s3)):
        part = pl.ds(b * 256, 256)
        total = own[part, :] + other[part, :].astype(F32) + g1[part, :].astype(F32)
        total = total + g2[part, :].astype(F32) + g3[part, :].astype(F32)
        out[...] = total.astype(out.dtype)


def second_sum(own, other, got):
    return pl.pallas_call(
        second_sum_kernel,
        out_shape=(sds((256, 128), F32),) + (sds((256, 128), BF),) * 3,
        in_specs=[VM] * 5,
        out_specs=(VM,) * 4,
        name="second_sum",
        compiler_params=PARAMS,
    )(own, other, *got)


def middle_kernel(own, g1, g3, g2, weight, cotangent, out, message):
    mixed = own[...] + g1[...].astype(F32) + g2[...].astype(F32) + g3[...].astype(F32)
    high, low = split(mixed)
    w = weight[...]
    summed = dot(high, w) + dot(low, w)
    gate = 1.0 / (1.0 + jnp.exp(-summed))
    out[...] = summed * gate
    slope = gate * (1.0 + summed * (1.0 - gate))
    grad = (cotangent[...].astype(F32) * slope).astype(BF)
    back = lax.dot_general(w, grad, (((1,), (1,)), ((), ())), preferred_element_type=F32)
    message[0] = back.astype(BF)
    over_rows = (((0,), (0,)), ((), ()))
    term = lax.dot_general(high, grad, over_rows, preferred_element_type=F32)
    term = term + lax.dot_general(low, grad, over_rows, preferred_element_type=F32)
    message[1], message[2] = split(term)


def middle(own, got, weight, cotangent):
    return pl.pallas_call(
        middle_kernel,
        out_shape=(sds((256, 256), F32), sds((3, 128, 256), BF)),
        in_specs=[VM] * 6,
        out_specs=(VM,) * 2,
        name="middle",
        compiler_params=PARAMS,
    )(own, *got, weight, cotangent)


def ring_sum(own, g1, g2, g3, at, terms=2):
    own, g1, g2, g3 = [joined(ref, at, terms) for ref in (own, g1, g2, g3)]
    return (own + g2) + (g1 + g3)


def gather_kernel(own, g3, g1, g2, message):
    for b, ref in enumerate((own, g1, g2, g3)):
        message[b] = ref[0]
    for n, term in enumerate(split(ring_sum(own, g1, g2, g3, 1), COL_TERMS)):
        message[4 + n] = term


def gather_step(own, got):
    return pl.pallas_call(
        gather_kernel,
        out_shape=sds((4 + COL_TERMS, 128, 256), BF),
        in_specs=[VM] * 4,
        out_specs=VM,
        name="gather_step",
        compiler_params=PARAMS,
    )(own, *got)


def backward_tiles(half, a, q, table, values, part, total):
    for b in range(4):
        base = (half * 32 + a * 8 + b * 2) * 8 + 2 * q
        upper = [tile(values, table[base]), tile(values, table[base + 1])]
        lower = [tile(values, table[base + 8]), tile(values, table[base + 9])]
        block = jnp.concatenate(
            [jnp.concatenate(upper, axis=1), jnp.concatenate(lower, axis=1)], axis=0
        )
        term = dot(part[b], block)
        total = term if total is None else total + term
    return total


def backward_kernel(half, offsets, first, table, values, *refs):
    parts, out = refs[: len(offsets)], refs[-1]
    for q in range(4):
        total = None if first else refs[len(offsets)][q]
        for a, part in zip(offsets, parts):
            total = backward_tiles(half, a, q, table, values, part, total)
        out[q] = total


BACK_COST = pl.CostEstimate(flops=1, bytes_accessed=1, transcendentals=0)


def backward(half, offsets, table, values, parts, partial):
    given = () if partial is None else (partial,)
    return pl.pallas_call(
        functools.partial(backward_kernel, half, offsets, partial is None),
        out_shape=sds((4, 128, 256), F32),
        in_specs=[SM] + [VM] * (1 + len(parts) + len(given)),
        out_specs=VM,
        name=f"backward_{half}_{offsets[0]}",
        cost_estimate=BACK_COST,
        compiler_params=PARAMS,
    )(table, values, *parts, *given)


def backward_first_kernel(table, values, part, active, out, output):
    for q in range(4):
        out[q] = backward_tiles(1, 0, q, table, values, part, None)
    output[...] = active[...].astype(BF)


def backward_first(table, values, part, active):
    return pl.pallas_call(
        backward_first_kernel,
        out_shape=(sds((4, 128, 256), F32), sds(active.shape, BF)),
        in_specs=[SM] + [VM] * 3,
        out_specs=(VM,) * 2,
        name="backward_first",
        cost_estimate=BACK_COST,
        compiler_params=PARAMS,
    )(table, values, part, active)


def tie_kernel(*refs):
    del refs


def tie(values, after):
    return pl.pallas_call(
        tie_kernel,
        out_shape=[sds(value.shape, value.dtype) for value in values],
        in_specs=[AN] * (len(values) + 1),
        out_specs=[AN] * len(values),
        input_output_aliases={n: n for n in range(len(values))},
        name="tie",
        compiler_params=PARAMS,
    )(*values, after)


def last_kernel(half, offsets, table, values, p0, p3, p1, p2, o0, o3, o1, o2, partial, own_term, s3, s1, s2):
    sends = (s1, s2, s3)
    parts = [(o0, o1, o2, o3)[a] for a in offsets]
    term = ring_sum(p0, p1, p2, p3, 4, COL_TERMS) + ring_sum(o0, o1, o2, o3, 4, COL_TERMS)
    for n, term in enumerate(split(term, ROW_TERMS)):
        own_term[n] = term
        for out in sends:
            out[1 + n] = term
    for q in range(1, 4):
        total = partial[q]
        for a, part in zip(offsets, parts):
            total = backward_tiles(half, a, q, table, values, part, total)
        sends[q - 1][0] = total.astype(BF)


def last(half, offsets, table, values, mine, others, partial):
    return pl.pallas_call(
        functools.partial(last_kernel, half, offsets),
        out_shape=(sds((ROW_TERMS, 128, 256), BF),) + (sds((1 + ROW_TERMS, 128, 256), BF),) * 3,
        in_specs=[SM] + [VM] * 10,
        out_specs=(VM,) * 4,
        name="backward_last",
        cost_estimate=BACK_COST,
        compiler_params=PARAMS,
    )(table, values, *mine, *others, partial)


def kept_kernel(half, offset, table, values, part, partial, after, own):
    del after
    own[...] = backward_tiles(half, offset, 0, table, values, part, partial[0])


def kept_quarter(half, offset, table, values, part, partial, after):
    return pl.pallas_call(
        functools.partial(kept_kernel, half, offset),
        out_shape=sds((128, 256), F32),
        in_specs=[SM] + [VM] * 3 + [AN],
        out_specs=VM,
        name="backward_kept",
        cost_estimate=BACK_COST,
        compiler_params=PARAMS,
    )(table, values, part, partial, after)


def finish_kernel(scale, own, own_term, g3, g1, g2, grad_in, grad_weight):
    total = own[...] + g1[0].astype(F32) + g2[0].astype(F32) + g3[0].astype(F32)
    grad_in[...] = total.T.astype(BF)
    g1, g2, g3 = [joined(ref, 1, ROW_TERMS) for ref in (g1, g2, g3)]
    term = (joined(own_term, 0, ROW_TERMS) + g2) + (g1 + g3)
    grad_weight[...] = term * scale


def finish(scale, own, own_term, got):
    return pl.pallas_call(
        functools.partial(finish_kernel, scale),
        out_shape=(sds((256, 128), BF), sds((128, 256), F32)),
        in_specs=[VM] * 5,
        out_specs=(VM,) * 2,
        name="finish",
        compiler_params=PARAMS,
    )(own, own_term, *got)


def row_shift(value, k):
    return lax.ppermute(value, "row", [(i, (i + k) % 4) for i in range(4)])


def swap_cores(value):
    return lax.ppermute(value, "col", [(j, j ^ 1) for j in range(32)])


def chip_shift(value, k, x_core):
    pairs = []
    for z in range(4):
        for x in range(4):
            for core in range(2):
                if core == x_core:
                    to = (z, (x + k) % 4)
                else:
                    to = ((z + k) % 4, x)
                pairs.append(((z * 4 + x) * 2 + core, (to[0] * 4 + to[1]) * 2 + core))
    return lax.ppermute(value, "col", pairs)


ORDER = {1: (1, 3, 2), -1: (3, 1, 2)}


def shift_each(shift, values, sign, *args):
    return [shift(v, sign * k, *args) for k, v in zip(ORDER[sign], values)]


def local(features, weight, cotangent, tile_values, tile_rows, tile_cols, tile_counts):
    shifted = shift_each(row_shift, [features] * 3, 1)
    values, own_features, table = load(
        tile_values[0, 0], features, tile_rows, tile_cols, tile_counts
    )
    sources = [own_features] + shifted
    other = swap_cores(forward("forward_other", 8, 24, BF, table, values, sources))
    sent = forward("forward_sent", 40, 24, F32, table, values, sources)
    got = shift_each(chip_shift, first_sum(sent, other), 1, 0)
    other = swap_cores(forward("forward_rest", 0, 8, BF, table, values, sources, sent))
    kept = forward("forward_kept", 32, 8, F32, table, values, sources)
    own, *sends = second_sum(kept, other, got)
    got = shift_each(chip_shift, sends, 1, 1)
    active, message = middle(own, got, weight, cotangent)
    got = shift_each(chip_shift, [message] * 3, -1, 1)
    message = gather_step(message, got)
    first = message
    rest = shift_each(chip_shift, [message] * 3, -1, 0)
    other_first = swap_cores(first)
    partial, output = backward_first(table, values, first, active)
    partial = backward(0, (0,), table, values, (other_first,), partial)
    rest = tie(rest, partial)
    other_rest = [swap_cores(v) for v in rest]
    partial = backward(1, ORDER[-1], table, values, rest, partial)
    mine, others = (first, *rest), (other_first, *other_rest)
    partial = backward(0, ORDER[-1][:2], table, values, other_rest[:2], partial)
    own_term, *sends = last(0, ORDER[-1][2:], table, values, mine, others, partial)
    own = kept_quarter(0, ORDER[-1][2], table, values, other_rest[2], partial, own_term)
    got = shift_each(row_shift, sends, -1)
    grad_in, grad_weight = finish(32768.0 ** -0.5, own, own_term, got)
    return output, grad_in, grad_weight


def solution(mesh):
    placed = (
        P(("row", "col"), None),
        P(),
        P(("row", "col"), None),
        P("row", "col", None, None, None),
        P("row", "col", None),
        P("row", "col", None),
        P("row", "col"),
    )
    return jax.shard_map(
        local,
        mesh=mesh,
        in_specs=placed,
        out_specs=(P(("row", "col"), None), P(("row", "col"), None), P()),
        check_vma=False,
    )
```
